1024 devices in a mesh: expert: 64 (over y, x), tensor: 16 (over z, core).
Axes of the slice: x: 8, y: 8, z: 8, core: 2. Of those that a mesh axis runs over, the one named last changes fastest.
Arguments:
- tokens: bfloat16 [8192, 2048], P('expert', 'tensor')
- norm_gain: float32 [2048], replicated, may hold values from 0.5 to 1.5
- picks: int32 [32, 512], replicated, may hold values from 0 to 8191, as said below
- gates: float32 [32, 512], replicated, may hold values from 0.1 to 1
- shared_gate: bfloat16 [2048, 2048], P(None, 'tensor'), may hold values from -0.125 to 0.125
- shared_up: bfloat16 [2048, 2048], P(None, 'tensor'), may hold values from -0.125 to 0.125
- shared_down: bfloat16 [2048, 2048], P('tensor'), may hold values from -0.125 to 0.125
- expert_in: bfloat16 [64, 2048, 4096], P('expert', None, 'tensor'), may hold values from -0.125 to 0.125
- expert_out: bfloat16 [64, 4096, 2048], P('expert', 'tensor'), may hold values from -0.0625 to 0.0625
Outputs:
- mixed: bfloat16 [8192, 2048], P('expert', 'tensor')
The draws below stay inside these ranges and needn't reach their ends.
Inputs may be any that keep to these rules, and one draw needn't show every extreme that they name: Each expert's list names 512 different tokens. Calling tokens 128 * s to 128 * s + 127 group s, at most 16 of one expert's picks lie in one group, and every expert's list has exactly 16 in some group.
All inputs are finite; a program needn't handle non-finite values.
Results may differ from the reference program's by a relative error of at most 0.024.
Values may be sent and summed in bfloat16 or wider, within the bound.
A program may use at most 32 MiB of HBM per device.

```python
import math
import jax
import jax.numpy as jnp
from jax import lax

D = 2048
FF = 8192
SH = 2048
TOK_GRP = 128
EXPERTS = 32
TOKENS = 8192
CAP = 512
MOST = 16
N_TENSOR = 16


def draw_tokens(key, part):
    key = jax.random.fold_in(key, 11)
    key_base, key_cols, key_rows = jax.random.split(key, 3)
    rising = 3.0 ** (jnp.arange(D, dtype=jnp.float32) / (D - 1))
    column_scale = rising * jnp.exp(jax.random.uniform(key_cols, (D,), jnp.float32, 0.0, math.log(10.0))) / 4.0
    baseline = jax.random.normal(key_base, (TOKENS, D), jnp.float32)
    row_scale = jnp.exp(jax.random.uniform(key_rows, (TOKENS, 1), jnp.float32, 0.0, math.log(10.0)))
    values = baseline * column_scale * row_scale / 3.0
    return values.astype(jnp.bfloat16)


def draw_picks(key, part):
    key = jax.random.fold_in(key, 23)
    key_hot, key_order, key_rows, key_mix = jax.random.split(key, 4)
    holders = TOKENS // TOK_GRP
    hot_limit = max(holders // 8, 1)
    hot_count = jax.random.randint(key_hot, (EXPERTS, 1), 1, hot_limit + 1)
    remainder = CAP - hot_count * MOST
    baseline = remainder // (holders - hot_count)
    surplus = remainder - baseline * (holders - hot_count)
    ranks = jnp.arange(holders, dtype=jnp.int32)[None, :]
    counts = jnp.where(ranks < hot_count, MOST, baseline + (ranks - hot_count < surplus).astype(jnp.int32))
    ends = jnp.cumsum(counts, axis=1)
    starts = ends - counts
    owner_order = jax.vmap(lambda subkey: jax.random.permutation(subkey, holders))(jax.random.split(key_order, EXPERTS))
    row_orders = jax.vmap(lambda subkey: jax.random.permutation(subkey, TOK_GRP))(jax.random.split(key_rows, EXPERTS * holders))
    row_orders = row_orders.reshape(EXPERTS, holders * TOK_GRP)
    positions = jnp.arange(CAP, dtype=jnp.int32)
    rank_of = jnp.sum((ends[:, None, :] <= positions[None, :, None]).astype(jnp.int32), axis=2)
    within = positions[None, :] - jnp.take_along_axis(starts, rank_of, axis=1)
    owners = jnp.take_along_axis(owner_order, rank_of, axis=1)
    local_rows = jnp.take_along_axis(row_orders, rank_of * TOK_GRP + within, axis=1)
    listed = owners * TOK_GRP + local_rows
    mixing = jax.vmap(lambda subkey: jax.random.permutation(subkey, CAP))(jax.random.split(key_mix, EXPERTS))
    return jnp.take_along_axis(listed, mixing, axis=1).astype(jnp.int32)


def block_levels(stream_key, dims, cuts, least, high):
    level, own = 1.0, jax.random.fold_in(stream_key, 6)
    for dim, shards_of in cuts:
        steps = jnp.exp(jax.random.uniform(jax.random.fold_in(own, dim), (shards_of,), jnp.float32, least / len(cuts), high / len(cuts)))
        level = level * jnp.repeat(steps, dims[dim] // shards_of).reshape([-1 if axis == dim else 1 for axis in range(len(dims))])
    return level


def gaussian(stream_key, dims, spread, most, pieces=(), held_as=jnp.bfloat16):
    array = jax.random.normal(stream_key, dims, jnp.float32) * spread
    if len(pieces) > 0:
        array = block_levels(stream_key, dims, pieces, -0.22, 0.18) * array
    return jnp.clip(array, min=-most, max=most).astype(held_as)


def setup_inputs(seed: int = 0) -> dict:
    streams_of = jax.random.split(jax.random.key(seed), 10)
    return {
        "tokens": draw_tokens(jax.random.fold_in(streams_of[9], 71), 0),
        "norm_gain": jnp.clip(jax.random.uniform(streams_of[1], (D,), jnp.float32, 0.5, 1.5), 0.5, 1.5),
        "picks": draw_picks(jax.random.fold_in(streams_of[9], 71), 0),
        "gates": jnp.clip(jnp.exp(jax.random.uniform(streams_of[3], (EXPERTS, CAP), jnp.float32, math.log(0.1), math.log(1.0))), 0.1, 1.0),
        "shared_gate": gaussian(streams_of[4], (D, SH), D ** -0.5, 0.125, ((1, 16),)),
        "shared_up": gaussian(streams_of[5], (D, SH), D ** -0.5, 0.125, ((1, 16),)),
        "shared_down": gaussian(streams_of[6], (SH, D), SH ** -0.5, 0.125, ((0, 16),)),
        "expert_in": gaussian(streams_of[7], (2 * EXPERTS, D, FF // 2), D ** -0.5, 0.125, ((0, 64), (2, 16))),
        "expert_out": gaussian(streams_of[8], (2 * EXPERTS, FF // 2, D), FF ** -0.5, 0.0625, ((0, 64), (1, 16))),
    }


EPS = 1e-06

def sliced_sum(hidden, weights, sections):
    stride_units = hidden.shape[1] // sections
    running = jnp.zeros((hidden.shape[0], weights.shape[1]), jnp.float32)
    for section in range(sections):
        partial_term = jnp.dot(hidden[:, section * stride_units:(section + 1) * stride_units], weights[section * stride_units:(section + 1) * stride_units], preferred_element_type=jnp.float32)
        rounded = lax.optimization_barrier(partial_term.astype(jnp.bfloat16))
        running = running + rounded.astype(jnp.float32)
    return running

def reference(tokens, norm_gain, picks, gates, shared_gate, shared_up, shared_down, expert_in, expert_out):
    widened = tokens.astype(jnp.float32)
    scaled = (widened * norm_gain).astype(jnp.bfloat16)
    inverse = lax.rsqrt(lax.optimization_barrier(jnp.mean(widened * widened, axis=1)) + EPS)
    gate_part = inverse[:, None] * jnp.dot(scaled, shared_gate, preferred_element_type=jnp.float32)
    up_part = inverse[:, None] * jnp.dot(scaled, shared_up, preferred_element_type=jnp.float32)
    shared_hidden = (jax.nn.silu(gate_part) * up_part).astype(jnp.bfloat16)
    shared_sums = sliced_sum(shared_hidden, shared_down, N_TENSOR)
    picks_both = jnp.repeat(picks, 2, axis=0)
    gates_both = jnp.repeat(gates, 2, axis=0)

    def one_half(operands):
        chosen, weights_in, weights_out, gate_values = operands
        picked_rows = jnp.take(scaled, chosen, axis=0)
        hidden = inverse[chosen][:, None] * jnp.dot(picked_rows, weights_in, preferred_element_type=jnp.float32)
        activation = jax.nn.gelu(hidden, approximate=False).astype(jnp.bfloat16)
        summed = sliced_sum(activation, weights_out, N_TENSOR)
        return (gate_values[:, None] * summed).astype(jnp.bfloat16)
    gated = lax.map(one_half, (picks_both, expert_in, expert_out, gates_both))
    mixture = jnp.zeros((tokens.shape[0], tokens.shape[1]), jnp.float32).at[picks_both.reshape(-1)].add(gated.reshape(-1, tokens.shape[1]).astype(jnp.float32))
    return (shared_sums + mixture).astype(jnp.bfloat16)
```

```python
import jax
import jax.numpy as jnp
from jax import lax
from jax.experimental import pallas as pl
from jax.experimental.pallas import tpu as pltpu
from jax.sharding import PartitionSpec as P

EPS = 1e-06
BF = jnp.bfloat16
F32 = jnp.float32
MESH = pl.DeviceIdType.MESH
FAR_FIRST = (4, 3, 5, 2, 6, 1, 7)
ROOT_HALF = 0.7071067811865476


def one_hot(condition):
    return jnp.where(condition, 1.0, 0.0).astype(BF)


def dot(a, b):
    return jnp.dot(a, b, preferred_element_type=F32)


def wait_bytes(ref, sem):
    pltpu.make_async_copy(ref, ref, sem).wait()


def layer(
    tokens_hbm, gain_hbm, picks_hbm, gates_hbm, gate_hbm, up_hbm, down_hbm, in_hbm, out_hbm,
    result,
    tokens, gain, picks, gates, w_gate_up, w_down, w_in, w_out,
    selector, outgoing, mid, slots, picker, picker_t, gate_wide,
    own_tokens, shared_part, shared_sib, shared_send, shared_recv,
    gathered, hidden, squares, activation, partial, partial_sib, ring_send, ring_recv,
    expanded, ret_x, ret_mid, ret_y,
    load_sem, a2a_send, a2a_recv, tok_send, tok_recv, sib_send, sib_recv,
    ag_send, ag_recv, agsib_send, agsib_recv, rs_send, rs_recv, rssib_send, rssib_recv,
):
    e = lax.axis_index("expert")
    t = lax.axis_index("tensor")
    y, x = e // 8, e % 8
    z, c = t // 2, t % 2
    other = 1 - c
    half_rows = 256

    def at_y(k):
        return (((y + k) % 8) * 8 + x, t)

    def at_x(k):
        return (y * 8 + (x + k) % 8, t)

    def at_z(k):
        return (e, ((z + k) % 8) * 2 + c)

    sibling = (e, z * 2 + other)

    def remote(src, dst, send, recv, device):
        copy = pltpu.make_async_remote_copy(
            src, dst, send, recv, device_id=device, device_id_type=MESH
        )
        copy.start()
        return copy

    loads = [
        pltpu.make_async_copy(src, dst, load_sem.at[n])
        for n, (src, dst) in enumerate(
            [
                (picks_hbm, picks),
                (tokens_hbm, tokens),
                (gain_hbm, gain),
                (gates_hbm, gates),
                (gate_hbm, w_gate_up.at[:, pl.ds(0, 128)]),
                (up_hbm, w_gate_up.at[:, pl.ds(128, 128)]),
                (down_hbm, w_down),
                (in_hbm.at[0], w_in),
                (out_hbm.at[0], w_out),
            ]
        )
    ]
    for load in loads:
        load.start()

    barrier = pltpu.get_barrier_semaphore()
    for k in range(1, 8):
        for device in (at_y(k), at_x(k), at_z(k)):
            pl.semaphore_signal(barrier, inc=1, device_id=device, device_id_type=MESH)
    pl.semaphore_signal(barrier, inc=1, device_id=sibling, device_id_type=MESH)

    triangle = one_hot(
        lax.broadcasted_iota(jnp.int32, (512, 512), 0)
        <= lax.broadcasted_iota(jnp.int32, (512, 512), 1)
    )
    loads[0].wait()
    all_picks = picks[...]
    mine = (all_picks >> 7) == e
    rank = dot(one_hot(mine), triangle)
    rank = jnp.where(mine, rank, 0.0)
    local = (all_picks & 127).astype(F32) + 1.0
    slot_number = lax.broadcasted_iota(jnp.int32, (16, 512), 0).astype(F32) + 1.0
    row_number = lax.broadcasted_iota(jnp.int32, (16, 128), 1).astype(F32) + 1.0
    for n in range(32):
        matched = jnp.where(rank[n : n + 1, :] == slot_number, local[n : n + 1, :], 0.0)
        row = jnp.sum(matched, axis=1, keepdims=True)
        selector[n * 16 : (n + 1) * 16, :] = one_hot(row == row_number)
    loads[1].wait()
    out_rows = dot(selector[...], tokens[...]).astype(BF)
    outgoing[...] = out_rows.reshape(8, 64, 128)
    own_tokens[c, z] = tokens[...]
    mid[y] = outgoing[y]

    pl.semaphore_wait(barrier, 22)

    waits_send = []
    for k in FAR_FIRST:
        waits_send.append(
            remote(outgoing.at[(y + k) % 8], mid.at[y], a2a_send.at[0], a2a_recv.at[0], at_y(k))
        )
    tok_copies = [
        remote(own_tokens.at[c, z], own_tokens.at[c, z], tok_send.at[0], tok_recv.at[0], at_z(k))
        for k in FAR_FIRST
    ]

    chosen = picks[pl.ds(e // 2, 1), :]
    anchor = chosen >> 7
    from_group = anchor == lax.broadcasted_iota(jnp.int32, (64, 512), 0)
    counts = dot(one_hot(from_group), triangle)
    order = jnp.sum(jnp.where(from_group, counts, 0.0), axis=0, keepdims=True) - 1.0
    slot = (((anchor & 7) * 8 + (anchor >> 3)) * 16).astype(F32) + order

    wait_bytes(mid.at[pl.ds(0, 7)], a2a_recv.at[0])
    for k in FAR_FIRST:
        waits_send.append(
            remote(
                mid.at[:, pl.ds(((x + k) % 8) // 2 * 16, 16), :],
                slots.at[x],
                a2a_send.at[1],
                a2a_recv.at[1],
                at_x(k),
            )
        )
    slots[x] = mid[:, pl.ds(pl.multiple_of(x // 2 * 16, 16), 16), :]

    slot_wide = jnp.transpose(jnp.broadcast_to(slot, (128, 512)))
    lane = lax.broadcasted_iota(jnp.int32, (512, 128), 1).astype(F32)
    sublane = lax.broadcasted_iota(jnp.int32, (128, 512), 0).astype(F32)
    for b in range(8):
        picker[:, b * 128 : (b + 1) * 128] = one_hot(slot_wide == lane + b * 128.0)

    wait_bytes(own_tokens.at[0, pl.ds(0, 7)], tok_recv.at[0])
    tok_sib = remote(own_tokens.at[c], own_tokens.at[c], sib_send.at[0], sib_recv.at[0], sibling)

    def ag_copy(d, k, h):
        src = (z - k + 8) % 8 if d == 0 else (z + k) % 8
        ref = gathered.at[c, src, pl.ds(h * half_rows, half_rows)]
        return remote(ref, ref, ag_send.at[d, k, h], ag_recv.at[d, k, h], at_z(1 if d == 0 else 7))

    def ag_sib(src, h, n):
        ref = gathered.at[c, src, pl.ds(h * half_rows, half_rows)]
        return remote(ref, ref, agsib_send.at[n, h], agsib_recv.at[n, h], sibling)

    wait_bytes(slots.at[pl.ds(0, 7)], a2a_recv.at[1])
    ag_copies = []
    sib_copies = []
    for h in (0, 1):
        rows = pl.ds(h * half_rows, half_rows)
        gathered[c, z, rows] = dot(picker[rows, :], slots[...].reshape(1024, 128)).astype(BF)
        for d in (0, 1):
            ag_copies.append(ag_copy(d, 0, h))
        sib_copies.append(ag_sib(z, h, 0))

    for b in range(8):
        picker_t[b * 128 : (b + 1) * 128, :] = one_hot(slot == sublane + b * 128.0)
    loads[3].wait()
    gate_wide[...] = jnp.transpose(jnp.broadcast_to(gates[pl.ds(e // 2, 1), :], (128, 512)))
    loads[2].wait()

    def shared_branch():
        wait_bytes(own_tokens.at[other], sib_recv.at[0])
        for load in loads[4:7]:
            load.wait()
        scaled = []
        total = jnp.zeros((128, 128), F32)
        for n in range(16):
            wide = own_tokens[n % 2, n // 2].astype(F32)
            scaled.append((wide * gain[n : n + 1, :]).astype(BF))
            total = total + wide * wide
        inverse = lax.rsqrt(jnp.sum(total, axis=1, keepdims=True) / 2048.0 + EPS)
        both = inverse * dot(jnp.concatenate(scaled, axis=1), w_gate_up[...])
        gate_part = both[:, :128]
        shared_hidden = (gate_part / (1.0 + jnp.exp(-gate_part)) * both[:, 128:]).astype(BF)
        for n in range(16):
            term = dot(shared_hidden, w_down[:, n * 128 : (n + 1) * 128])
            shared_part[n % 2, n // 2] = term.astype(BF)
        return remote(
            shared_part.at[other], shared_sib, sib_send.at[1], sib_recv.at[1], sibling
        )

    def absorb(h, chunks, first=False):
        rows = pl.ds(h * half_rows, half_rows)
        scaled = []
        weights = []
        total = None
        for plane, src in chunks:
            feature = src * 2 + plane
            wide = gathered[plane, src, rows].astype(F32)
            scaled.append((wide * gain[pl.ds(feature, 1), :]).astype(BF))
            weights.append(w_in[pl.ds(pl.multiple_of(feature * 128, 128), 128), :])
            total = wide * wide if total is None else total + wide * wide
        product = dot(jnp.concatenate(scaled, axis=1), jnp.concatenate(weights, axis=0))
        if first:
            hidden[rows, :] = product
            squares[rows, :] = total
        else:
            hidden[rows, :] += product
            squares[rows, :] += total

    def sib_wait(src, h, n):
        wait_bytes(gathered.at[other, src, pl.ds(h * half_rows, half_rows)], agsib_recv.at[n, h])

    shared_copy = shared_branch()
    loads[7].wait()
    for h in (0, 1):
        sib_wait(z, h, 0)
        absorb(h, [(c, z), (other, z)], first=True)

    def ag_from(d, k):
        return (z + 7 - k) % 8 if d == 0 else (z + 1 + k) % 8

    previous = None
    for k in range(4):
        for hh in (0, 1):
            pair = [(0, hh), (1, 1 - hh)]
            if k == 3 and hh == 1:
                continue
            for d, h in pair:
                src = ag_from(d, k)
                wait_bytes(
                    gathered.at[c, src, pl.ds(h * half_rows, half_rows)], ag_recv.at[d, k, h]
                )
                if k < 2 or (k == 2 and hh == 0):
                    ag_copies.append(ag_copy(d, k + 1, h))
                sib_copies.append(ag_sib(src, h, 1 + k * 2 + d if k < 3 else 7))
        if previous is not None:
            for h in (0, 1):
                for d in (0, 1):
                    sib_wait(ag_from(d, previous), h, 1 + previous * 2 + d)
                absorb(h, [(p, ag_from(d, previous)) for d in (0, 1) for p in (c, other)])
        previous = k
    last = ag_from(0, 3)
    loads[8].wait()
    for h in (0, 1):
        rows = pl.ds(h * half_rows, half_rows)
        sib_wait(last, h, 7)
        absorb(h, [(c, last), (other, last)])
        inverse = lax.rsqrt(jnp.sum(squares[rows, :], axis=1, keepdims=True) / 2048.0 + EPS)
        value = inverse * hidden[rows, :]
        activation[rows, :] = (value * 0.5 * (1.0 + lax.erf(value * ROOT_HALF))).astype(BF)

    rs_copies = []

    def project(k):
        column = pl.multiple_of((z + k) % 8 * 256, 256)
        weight = w_out[:, pl.ds(column, 256)]
        for h in (0, 1):
            rows = pl.ds(h * half_rows, half_rows)
            term = dot(activation[rows, :], weight).astype(BF)
            partial[k, 0, rows] = term[:, :128]
            partial[k, 1, rows] = term[:, 128:]
        rs_copies.append(
            remote(
                partial.at[k, other], partial_sib.at[k], rssib_send.at[k], rssib_recv.at[k], sibling
            )
        )

    arrived = set()

    def chip_sum(k, h):
        if k not in arrived:
            arrived.add(k)
            wait_bytes(partial_sib.at[k], rssib_recv.at[k])
        rows = pl.ds(h * half_rows, half_rows)
        return partial[k, c, rows].astype(F32) + partial_sib[k, rows].astype(F32)

    def ring_in(d, k, h):
        wait_bytes(ring_recv.at[d, k - 1, h], rs_recv.at[d, k - 1, h])
        return ring_recv[d, k - 1, h].astype(F32)

    def ring_out(d, k, h, incoming=True):
        total = chip_sum(k if d == 0 else 8 - k, h)
        if incoming:
            total = total + ring_in(d, k + 1, h)
        ring_send[d, k - 1, h] = total.astype(BF)
        rs_copies.append(
            remote(
                ring_send.at[d, k - 1, h],
                ring_recv.at[d, k - 1, h],
                rs_send.at[d, k - 1, h],
                rs_recv.at[d, k - 1, h],
                at_z(1 if d == 0 else 7),
            )
        )

    project(4)
    project(3)
    project(5)
    for d in (0, 1):
        ring_out(d, 4, d, incoming=False)
    for d in (0, 1):
        ring_out(d, 3, 1 - d, incoming=False)
    project(2)
    project(6)
    for d in (0, 1):
        ring_out(d, 3, d)
    for d in (0, 1):
        ring_out(d, 2, 1 - d)
    project(1)
    project(7)
    project(0)
    for d in (0, 1):
        ring_out(d, 2, d)
    for d in (0, 1):
        ring_out(d, 1, 1 - d)
    for d in (0, 1):
        ring_out(d, 1, d)

    wait_bytes(shared_sib, sib_recv.at[1])
    shared_send[...] = (shared_part[c].astype(F32) + shared_sib[...].astype(F32)).astype(BF)

    gated = []
    for h in (1, 0):
        rows = pl.ds(h * half_rows, half_rows)
        total = chip_sum(0, h) + ring_in(0, 1, h) + ring_in(1, 1, h)
        gated.append((gate_wide[rows, :] * total).astype(BF))
    gated = jnp.concatenate([gated[1], gated[0]], axis=0)

    for k in FAR_FIRST + (0,):
        xx = (x + k) % 8
        block = picker_t[pl.ds(pl.multiple_of(xx * 128, 128), 128), :]
        expanded[xx] = dot(block, gated).astype(BF)
        if k == 0:
            ret_x[x] = expanded[x]
        else:
            waits_send.append(
                remote(expanded.at[xx], ret_x.at[x], a2a_send.at[2], a2a_recv.at[2], at_x(k))
            )
    for k in FAR_FIRST:
        waits_send.append(
            remote(
                shared_send.at[(z + k) % 8], shared_recv.at[z], tok_send.at[1], tok_recv.at[1], at_z(k)
            )
        )
    shared_recv[z] = shared_send[z]
    selector_t = lax.dot_general(
        one_hot(
            lax.broadcasted_iota(jnp.int32, (128, 128), 0)
            == lax.broadcasted_iota(jnp.int32, (128, 128), 1)
        ),
        selector[...],
        (((1,), (1,)), ((), ())),
        preferred_element_type=F32,
    ).astype(BF)

    wait_bytes(ret_x.at[pl.ds(0, 7)], a2a_recv.at[2])
    for j in range(4):
        added = ret_x[2 * j].astype(F32) + ret_x[2 * j + 1].astype(F32)
        ret_mid[:, j * 16 : (j + 1) * 16, :] = added.astype(BF).reshape(8, 16, 128)
    for k in FAR_FIRST:
        waits_send.append(
            remote(ret_mid.at[(y + k) % 8], ret_y.at[y], a2a_send.at[3], a2a_recv.at[3], at_y(k))
        )
    ret_y[y] = ret_mid[y]

    wait_bytes(shared_recv.at[pl.ds(0, 7)], tok_recv.at[1])
    total = shared_recv[0].astype(F32)
    for n in range(1, 8):
        total = total + shared_recv[n].astype(F32)
    wait_bytes(ret_y.at[pl.ds(0, 7)], a2a_recv.at[3])
    result[...] = (total + dot(selector_t, ret_y[...].reshape(512, 128))).astype(BF)

    for copy in waits_send + tok_copies + ag_copies + sib_copies + rs_copies:
        copy.wait_send()
    tok_sib.wait_send()
    shared_copy.wait_send()


def shards(
    tokens, norm_gain, picks, gates, shared_gate, shared_up, shared_down, expert_in, expert_out
):
    dma = pltpu.SemaphoreType.DMA
    vm = pltpu.VMEM
    return pl.pallas_call(
        layer,
        out_shape=jax.ShapeDtypeStruct((128, 128), BF),
        in_specs=[pl.BlockSpec(memory_space=pl.ANY)] * 9,
        out_specs=pl.BlockSpec(memory_space=pltpu.VMEM),
        scratch_shapes=[
            vm((128, 128), BF),
            vm((16, 128), F32),
            vm((32, 512), jnp.int32),
            vm((32, 512), F32),
            vm((2048, 256), BF),
            vm((128, 2048), BF),
            vm((2048, 256), BF),
            vm((256, 2048), BF),
            vm((512, 128), BF),
            vm((8, 64, 128), BF),
            vm((8, 64, 128), BF),
            vm((8, 8, 16, 128), BF),
            vm((512, 1024), BF),
            vm((1024, 512), BF),
            vm((512, 128), F32),
            vm((2, 8, 128, 128), BF),
            vm((2, 8, 128, 128), BF),
            vm((8, 128, 128), BF),
            vm((8, 128, 128), BF),
            vm((8, 128, 128), BF),
            vm((2, 8, 512, 128), BF),
            vm((512, 256), F32),
            vm((512, 128), F32),
            vm((512, 256), BF),
            vm((8, 2, 512, 128), BF),
            vm((8, 512, 128), BF),
            vm((2, 4, 2, 256, 128), BF),
            vm((2, 4, 2, 256, 128), BF),
            vm((8, 128, 128), BF),
            vm((8, 128, 128), BF),
            vm((8, 64, 128), BF),
            vm((8, 64, 128), BF),
            dma((9,)),
            dma((4,)),
            dma((4,)),
            dma((2,)),
            dma((2,)),
            dma((2,)),
            dma((2,)),
            dma((2, 4, 2)),
            dma((2, 4, 2)),
            dma((8, 2)),
            dma((8, 2)),
            dma((2, 4, 2)),
            dma((2, 4, 2)),
            dma((8,)),
            dma((8,)),
        ],
        compiler_params=pltpu.CompilerParams(
            collective_id=0, has_side_effects=True, vmem_limit_bytes=62 << 20
        ),
        cost_estimate=pl.CostEstimate(
            flops=1_500_000_000, bytes_accessed=4_000_000, transcendentals=200_000
        ),
    )(
        tokens,
        norm_gain.reshape(16, 128),
        picks,
        gates,
        shared_gate,
        shared_up,
        shared_down,
        expert_in,
        expert_out,
    )


def solution(mesh):
    placed = (
        P("expert", "tensor"),
        P(),
        P(),
        P(),
        P(None, "tensor"),
        P(None, "tensor"),
        P("tensor", None),
        P("expert", None, "tensor"),
        P("expert", "tensor", None),
    )
    return jax.shard_map(
        shards, mesh=mesh, in_specs=placed, out_specs=P("expert", "tensor"), check_vma=False
    )
```

```python
import jax
import jax.numpy as jnp
from jax import lax
from jax.experimental import pallas as pl
from jax.experimental.pallas import tpu as pltpu
from jax.sharding import PartitionSpec as P

EPS = 1e-06
BF = jnp.bfloat16
F32 = jnp.float32
MESH = pl.DeviceIdType.MESH
FAR_FIRST = (4, 3, 5, 2, 6, 1, 7)
ROOT_HALF = 0.7071067811865476


def one_hot(condition):
    return jnp.where(condition, 1.0, 0.0).astype(BF)


def dot(a, b):
    return jnp.dot(a, b, preferred_element_type=F32)


def wait_bytes(ref, sem):
    pltpu.make_async_copy(ref, ref, sem).wait()


def layer(
    tokens_hbm, gain_hbm, picks_hbm, gates_hbm, gate_hbm, up_hbm, down_hbm, in_hbm, out_hbm,
    result,
    tokens, gain, picks, gates, w_gate_up, w_down, w_in, w_out,
    selector, outgoing, mid, slots, picker, picker_t, gate_wide,
    own_tokens, shared_part, shared_sib, shared_send, shared_recv,
    gathered, hidden, squares, activation, partial, partial_sib, ring_send, ring_recv,
    expanded, ret_x, ret_mid, ret_y,
    load_sem, a2a_send, a2a_recv, tok_send, tok_recv, sib_send, sib_recv,
    ag_send, ag_recv, agsib_send, agsib_recv, rs_send, rs_recv, rssib_send, rssib_recv,
):
    e = lax.axis_index("expert")
    t = lax.axis_index("tensor")
    y, x = e // 8, e % 8
    z, c = t // 2, t % 2
    other = 1 - c
    half_rows = 256
    sub_rows = 128
    subs = ((0, 1, 2, 3), (2, 3, 0, 1))

    def at_y(k):
        return (((y + k) % 8) * 8 + x, t)

    def at_x(k):
        return (y * 8 + (x + k) % 8, t)

    def at_z(k):
        return (e, ((z + k) % 8) * 2 + c)

    sibling = (e, z * 2 + other)

    def remote(src, dst, send, recv, device):
        copy = pltpu.make_async_remote_copy(
            src, dst, send, recv, device_id=device, device_id_type=MESH
        )
        copy.start()
        return copy

    loads = [
        pltpu.make_async_copy(src, dst, load_sem.at[n])
        for n, (src, dst) in enumerate(
            [
                (picks_hbm, picks),
                (tokens_hbm, tokens),
                (gain_hbm, gain),
                (gates_hbm, gates),
                (gate_hbm, w_gate_up.at[:, pl.ds(0, 128)]),
                (up_hbm, w_gate_up.at[:, pl.ds(128, 128)]),
                (down_hbm, w_down),
                (in_hbm.at[0], w_in),
                (out_hbm.at[0], w_out),
            ]
        )
    ]
    for load in loads:
        load.start()

    barrier = pltpu.get_barrier_semaphore()
    for k in range(1, 8):
        for device in (at_y(k), at_x(k), at_z(k)):
            pl.semaphore_signal(barrier, inc=1, device_id=device, device_id_type=MESH)
    pl.semaphore_signal(barrier, inc=1, device_id=sibling, device_id_type=MESH)

    triangle = one_hot(
        lax.broadcasted_iota(jnp.int32, (512, 512), 0)
        <= lax.broadcasted_iota(jnp.int32, (512, 512), 1)
    )
    loads[0].wait()
    all_picks = picks[...]
    mine = (all_picks >> 7) == e
    rank = dot(one_hot(mine), triangle)
    rank = jnp.where(mine, rank, 0.0)
    local = (all_picks & 127).astype(F32) + 1.0
    slot_number = lax.broadcasted_iota(jnp.int32, (16, 512), 0).astype(F32) + 1.0
    row_number = lax.broadcasted_iota(jnp.int32, (16, 128), 1).astype(F32) + 1.0
    for n in range(32):
        matched = jnp.where(rank[n : n + 1, :] == slot_number, local[n : n + 1, :], 0.0)
        row = jnp.sum(matched, axis=1, keepdims=True)
        selector[n * 16 : (n + 1) * 16, :] = one_hot(row == row_number)
    loads[1].wait()
    out_rows = dot(selector[...], tokens[...]).astype(BF)
    outgoing[...] = out_rows.reshape(8, 64, 128)
    own_tokens[c, z] = tokens[...]
    mid[y] = outgoing[y]

    pl.semaphore_wait(barrier, 22)

    waits_send = []
    for k in FAR_FIRST:
        waits_send.append(
            remote(outgoing.at[(y + k) % 8], mid.at[y], a2a_send.at[0], a2a_recv.at[0], at_y(k))
        )
    tok_copies = [
        remote(own_tokens.at[c, z], own_tokens.at[c, z], tok_send.at[0], tok_recv.at[0], at_z(k))
        for k in FAR_FIRST
    ]

    chosen = picks[pl.ds(e // 2, 1), :]
    anchor = chosen >> 7
    from_group = anchor == lax.broadcasted_iota(jnp.int32, (64, 512), 0)
    counts = dot(one_hot(from_group), triangle)
    order = jnp.sum(jnp.where(from_group, counts, 0.0), axis=0, keepdims=True) - 1.0
    slot = (((anchor & 7) * 8 + (anchor >> 3)) * 16).astype(F32) + order

    wait_bytes(mid.at[pl.ds(0, 7)], a2a_recv.at[0])
    for k in FAR_FIRST:
        waits_send.append(
            remote(
                mid.at[:, pl.ds(((x + k) % 8) // 2 * 16, 16), :],
                slots.at[x],
                a2a_send.at[1],
                a2a_recv.at[1],
                at_x(k),
            )
        )
    slots[x] = mid[:, pl.ds(pl.multiple_of(x // 2 * 16, 16), 16), :]

    slot_wide = jnp.transpose(jnp.broadcast_to(slot, (128, 512)))
    lane = lax.broadcasted_iota(jnp.int32, (512, 128), 1).astype(F32)
    sublane = lax.broadcasted_iota(jnp.int32, (128, 512), 0).astype(F32)
    for b in range(8):
        picker[:, b * 128 : (b + 1) * 128] = one_hot(slot_wide == lane + b * 128.0)

    def ag_copy(d, k, h):
        src = (z - k + 8) % 8 if d == 0 else (z + k) % 8
        ref = gathered.at[c, src, pl.ds(h * half_rows, half_rows)]
        return remote(ref, ref, ag_send.at[d, k, h], ag_recv.at[d, k, h], at_z(1 if d == 0 else 7))

    def ag_sib(src, h, n):
        ref = gathered.at[c, src, pl.ds(h * half_rows, half_rows)]
        return remote(ref, ref, agsib_send.at[n, h], agsib_recv.at[n, h], sibling)

    wait_bytes(slots.at[pl.ds(0, 7)], a2a_recv.at[1])
    ag_copies = []
    sib_copies = []
    for h in (0, 1):
        rows = pl.ds(h * half_rows, half_rows)
        gathered[c, z, rows] = dot(picker[rows, :], slots[...].reshape(1024, 128)).astype(BF)
        for d in (0, 1):
            ag_copies.append(ag_copy(d, 0, h))
        sib_copies.append(ag_sib(z, h, 0))

    wait_bytes(own_tokens.at[0, pl.ds(0, 7)], tok_recv.at[0])
    tok_sib = remote(own_tokens.at[c], own_tokens.at[c], sib_send.at[0], sib_recv.at[0], sibling)

    for b in range(8):
        picker_t[b * 128 : (b + 1) * 128, :] = one_hot(slot == sublane + b * 128.0)
    loads[3].wait()
    gate_wide[...] = jnp.transpose(jnp.broadcast_to(gates[pl.ds(e // 2, 1), :], (128, 512)))
    loads[2].wait()

    def shared_branch():
        wait_bytes(own_tokens.at[other], sib_recv.at[0])
        for load in loads[4:7]:
            load.wait()
        scaled = []
        total = jnp.zeros((128, 128), F32)
        for n in range(16):
            wide = own_tokens[n % 2, n // 2].astype(F32)
            scaled.append((wide * gain[n : n + 1, :]).astype(BF))
            total = total + wide * wide
        inverse = lax.rsqrt(jnp.sum(total, axis=1, keepdims=True) / 2048.0 + EPS)
        both = inverse * dot(jnp.concatenate(scaled, axis=1), w_gate_up[...])
        gate_part = both[:, :128]
        shared_hidden = (gate_part / (1.0 + jnp.exp(-gate_part)) * both[:, 128:]).astype(BF)
        for n in range(16):
            term = dot(shared_hidden, w_down[:, n * 128 : (n + 1) * 128])
            shared_part[n % 2, n // 2] = term.astype(BF)
        return remote(
            shared_part.at[other], shared_sib, sib_send.at[1], sib_recv.at[1], sibling
        )

    def absorb(h, chunks, first=False):
        rows = pl.ds(h * half_rows, half_rows)
        scaled = []
        weights = []
        total = None
        for plane, src in chunks:
            feature = src * 2 + plane
            wide = gathered[plane, src, rows].astype(F32)
            scaled.append((wide * gain[pl.ds(feature, 1), :]).astype(BF))
            weights.append(w_in[pl.ds(pl.multiple_of(feature * 128, 128), 128), :])
            total = wide * wide if total is None else total + wide * wide
        product = dot(jnp.concatenate(scaled, axis=1), jnp.concatenate(weights, axis=0))
        if first:
            hidden[rows, :] = product
            squares[rows, :] = total
        else:
            hidden[rows, :] += product
            squares[rows, :] += total

    def sib_wait(src, h, n):
        wait_bytes(gathered.at[other, src, pl.ds(h * half_rows, half_rows)], agsib_recv.at[n, h])

    shared_copy = shared_branch()
    loads[7].wait()
    for h in (0, 1):
        sib_wait(z, h, 0)
        absorb(h, [(c, z), (other, z)], first=True)

    def ag_from(d, k):
        return (z + 7 - k) % 8 if d == 0 else (z + 1 + k) % 8

    previous = None
    for k in range(4):
        for hh in (0, 1):
            pair = [(0, hh), (1, 1 - hh)]
            if k == 3 and hh == 1:
                continue
            for d, h in pair:
                src = ag_from(d, k)
                wait_bytes(
                    gathered.at[c, src, pl.ds(h * half_rows, half_rows)], ag_recv.at[d, k, h]
                )
                if k < 2 or (k == 2 and hh == 0):
                    ag_copies.append(ag_copy(d, k + 1, h))
                sib_copies.append(ag_sib(src, h, 1 + k * 2 + d if k < 3 else 7))
        if previous is not None:
            for h in (0, 1):
                for d in (0, 1):
                    sib_wait(ag_from(d, previous), h, 1 + previous * 2 + d)
                absorb(h, [(p, ag_from(d, previous)) for d in (0, 1) for p in (c, other)])
        previous = k
    last = ag_from(0, 3)
    loads[8].wait()

    def activate(h):
        rows = pl.ds(h * half_rows, half_rows)
        sib_wait(last, h, 7)
        absorb(h, [(c, last), (other, last)])
        inverse = lax.rsqrt(jnp.sum(squares[rows, :], axis=1, keepdims=True) / 2048.0 + EPS)
        value = inverse * hidden[rows, :]
        activation[rows, :] = (value * 0.5 * (1.0 + lax.erf(value * ROOT_HALF))).astype(BF)

    rs_copies = []

    def project(k, h):
        column = pl.multiple_of((z + k) % 8 * 256, 256)
        rows = pl.ds(h * half_rows, half_rows)
        term = dot(activation[rows, :], w_out[:, pl.ds(column, 256)]).astype(BF)
        partial[k, 0, rows] = term[:, :128]
        partial[k, 1, rows] = term[:, 128:]
        rs_copies.append(
            remote(
                partial.at[k, other, rows],
                partial_sib.at[k, rows],
                rssib_send.at[k, h],
                rssib_recv.at[k, h],
                sibling,
            )
        )

    arrived = set()

    def chip_sum(k, s):
        h = s // 2
        if (k, h) not in arrived:
            arrived.add((k, h))
            wait_bytes(partial_sib.at[k, pl.ds(h * half_rows, half_rows)], rssib_recv.at[k, h])
        rows = pl.ds(s * sub_rows, sub_rows)
        return partial[k, c, rows].astype(F32) + partial_sib[k, rows].astype(F32)

    def ring_in(d, k, s):
        wait_bytes(ring_recv.at[d, k - 1, s], rs_recv.at[d, k - 1, s])
        return ring_recv[d, k - 1, s].astype(F32)

    def ring_out(d, k, s, incoming=True):
        total = chip_sum(k if d == 0 else 8 - k, s)
        if incoming:
            total = total + ring_in(d, k + 1, s)
        ring_send[d, k - 1, s] = total.astype(BF)
        rs_copies.append(
            remote(
                ring_send.at[d, k - 1, s],
                ring_recv.at[d, k - 1, s],
                rs_send.at[d, k - 1, s],
                rs_recv.at[d, k - 1, s],
                at_z(1 if d == 0 else 7),
            )
        )

    def ring_step(k, part, incoming=True):
        for i in (2 * part, 2 * part + 1):
            for d in (0, 1):
                ring_out(d, k, subs[d][i], incoming)

    activate(0)
    project(4, 0)
    project(5, 0)
    activate(1)
    project(4, 1)
    project(3, 1)
    ring_step(4, 0, incoming=False)
    project(3, 0)
    ring_step(3, 1, incoming=False)
    project(5, 1)
    project(2, 1)
    project(6, 0)
    ring_step(3, 0)
    project(2, 0)
    project(6, 1)
    ring_step(2, 1)
    project(1, 1)
    project(7, 0)
    ring_step(2, 0)
    project(1, 0)
    project(7, 1)
    ring_step(1, 1)
    project(0, 0)
    project(0, 1)
    ring_step(1, 0)

    wait_bytes(shared_sib, sib_recv.at[1])
    shared_send[...] = (shared_part[c].astype(F32) + shared_sib[...].astype(F32)).astype(BF)

    gated = [None] * 4
    for s in (2, 3, 0, 1):
        total = chip_sum(0, s) + ring_in(0, 1, s) + ring_in(1, 1, s)
        gated[s] = (gate_wide[s * sub_rows : (s + 1) * sub_rows, :] * total).astype(BF)
    gated = jnp.concatenate(gated, axis=0)

    for k in FAR_FIRST + (0,):
        xx = (x + k) % 8
        block = picker_t[pl.ds(pl.multiple_of(xx * 128, 128), 128), :]
        expanded[xx] = dot(block, gated).astype(BF)
        if k == 0:
            ret_x[x] = expanded[x]
        else:
            waits_send.append(
                remote(expanded.at[xx], ret_x.at[x], a2a_send.at[2], a2a_recv.at[2], at_x(k))
            )
    for k in FAR_FIRST:
        waits_send.append(
            remote(
                shared_send.at[(z + k) % 8], shared_recv.at[z], tok_send.at[1], tok_recv.at[1], at_z(k)
            )
        )
    shared_recv[z] = shared_send[z]
    selector_t = lax.dot_general(
        one_hot(
            lax.broadcasted_iota(jnp.int32, (128, 128), 0)
            == lax.broadcasted_iota(jnp.int32, (128, 128), 1)
        ),
        selector[...],
        (((1,), (1,)), ((), ())),
        preferred_element_type=F32,
    ).astype(BF)

    wait_bytes(mid.at[pl.ds(0, 7)], a2a_send.at[0])
    wait_bytes(slots.at[pl.ds(0, 7)], a2a_send.at[1])
    wait_bytes(own_tokens.at[0, pl.ds(0, 7)], tok_send.at[0])
    for copy in ag_copies + sib_copies + rs_copies:
        copy.wait_send()
    tok_sib.wait_send()
    shared_copy.wait_send()

    wait_bytes(ret_x.at[pl.ds(0, 7)], a2a_recv.at[2])
    for j in range(4):
        added = ret_x[2 * j].astype(F32) + ret_x[2 * j + 1].astype(F32)
        ret_mid[:, j * 16 : (j + 1) * 16, :] = added.astype(BF).reshape(8, 16, 128)
    for k in FAR_FIRST:
        waits_send.append(
            remote(ret_mid.at[(y + k) % 8], ret_y.at[y], a2a_send.at[3], a2a_recv.at[3], at_y(k))
        )
    ret_y[y] = ret_mid[y]

    wait_bytes(shared_recv.at[pl.ds(0, 7)], tok_recv.at[1])
    total = shared_recv[0].astype(F32)
    for n in range(1, 8):
        total = total + shared_recv[n].astype(F32)
    wait_bytes(ret_y.at[pl.ds(0, 7)], a2a_recv.at[3])
    result[...] = (total + dot(selector_t, ret_y[...].reshape(512, 128))).astype(BF)

    wait_bytes(ret_x.at[pl.ds(0, 7)], a2a_send.at[2])
    wait_bytes(ret_y.at[pl.ds(0, 7)], a2a_send.at[3])
    wait_bytes(shared_recv.at[pl.ds(0, 7)], tok_send.at[1])


def shards(
    tokens, norm_gain, picks, gates, shared_gate, shared_up, shared_down, expert_in, expert_out
):
    dma = pltpu.SemaphoreType.DMA
    vm = pltpu.VMEM
    return pl.pallas_call(
        layer,
        out_shape=jax.ShapeDtypeStruct((128, 128), BF),
        in_specs=[pl.BlockSpec(memory_space=pl.ANY)] * 9,
        out_specs=pl.BlockSpec(memory_space=pltpu.VMEM),
        scratch_shapes=[
            vm((128, 128), BF),
            vm((16, 128), F32),
            vm((32, 512), jnp.int32),
            vm((32, 512), F32),
            vm((2048, 256), BF),
            vm((128, 2048), BF),
            vm((2048, 256), BF),
            vm((256, 2048), BF),
            vm((512, 128), BF),
            vm((8, 64, 128), BF),
            vm((8, 64, 128), BF),
            vm((8, 8, 16, 128), BF),
            vm((512, 1024), BF),
            vm((1024, 512), BF),
            vm((512, 128), F32),
            vm((2, 8, 128, 128), BF),
            vm((2, 8, 128, 128), BF),
            vm((8, 128, 128), BF),
            vm((8, 128, 128), BF),
            vm((8, 128, 128), BF),
            vm((2, 8, 512, 128), BF),
            vm((512, 256), F32),
            vm((512, 128), F32),
            vm((512, 256), BF),
            vm((8, 2, 512, 128), BF),
            vm((8, 512, 128), BF),
            vm((2, 4, 4, 128, 128), BF),
            vm((2, 4, 4, 128, 128), BF),
            vm((8, 128, 128), BF),
            vm((8, 128, 128), BF),
            vm((8, 64, 128), BF),
            vm((8, 64, 128), BF),
            dma((9,)),
            dma((4,)),
            dma((4,)),
            dma((2,)),
            dma((2,)),
            dma((2,)),
            dma((2,)),
            dma((2, 4, 2)),
            dma((2, 4, 2)),
            dma((8, 2)),
            dma((8, 2)),
            dma((2, 4, 4)),
            dma((2, 4, 4)),
            dma((8, 2)),
            dma((8, 2)),
        ],
        compiler_params=pltpu.CompilerParams(
            collective_id=0, has_side_effects=True, vmem_limit_bytes=62 << 20
        ),
        cost_estimate=pl.CostEstimate(
            flops=1_500_000_000, bytes_accessed=4_000_000, transcendentals=200_000
        ),
    )(
        tokens,
        norm_gain.reshape(16, 128),
        picks,
        gates,
        shared_gate,
        shared_up,
        shared_down,
        expert_in,
        expert_out,
    )


def solution(mesh):
    placed = (
        P("expert", "tensor"),
        P(),
        P(),
        P(),
        P(None, "tensor"),
        P(None, "tensor"),
        P("tensor", None),
        P("expert", None, "tensor"),
        P("expert", "tensor", None),
    )
    return jax.shard_map(
        shards, mesh=mesh, in_specs=placed, out_specs=P("expert", "tensor"), check_vma=False
    )
```
